256 devices in a mesh: img: 32 (over z, y_hi, core), txt: 8 (over y_lo, x).
Axes of the slice: x: 4, y: 4 (y_hi: 2, y_lo: 2; y = y_hi * 2 + y_lo), z: 8, core: 2. Of those that a mesh axis runs over, the one named last changes fastest.
Arguments:
- img_hidden: bfloat16 [16384, 1152], P(('img', 'txt')), may hold values from -6 to 6
- txt_hidden: bfloat16 [16384, 1152], P(('img', 'txt')), may hold values from -6 to 6
- img_labels: int32 [16384], P(('img', 'txt')), may hold values from 0 to 16383, each once
- txt_labels: int32 [16384], P(('img', 'txt')), may hold values from 0 to 16383, each once
- img_gain: float32 [1152], replicated, may hold values from 0.1 to 1.9
- img_shift: float32 [1152], replicated, may hold values from -3 to 3
- txt_gain: float32 [1152], replicated, may hold values from 0.1 to 1.9
- txt_shift: float32 [1152], replicated, may hold values from -3 to 3
- img_weight: bfloat16 [1152, 1152], replicated, may hold values from -0.1875 to 0.1875
- txt_weight: bfloat16 [1152, 1152], replicated, may hold values from -0.1875 to 0.1875
- logit_scale: float32 [1], replicated, may hold values from 90 to 110
- logit_bias: float32 [1], replicated, may hold values from -10.5 to -9.5
- loss_scale: float32 [1], replicated, may hold values from 16 to 64
- row_moment: float32 [2, 1152], P(None, 'txt'), may hold values from 10000000 to 1000000000
- col_moment: float32 [2, 1152], replicated, may hold values from 10000000 to 1000000000
Outputs:
- img_grad: bfloat16 [16384, 1152], P(('img', 'txt'))
- txt_grad: bfloat16 [16384, 1152], P(('img', 'txt'))
- update: float32 [1152, 2304], P('txt')
- row_new: float32 [2, 1152], P(None, 'txt')
- col_new: float32 [2, 1152], replicated
The draws below stay inside these ranges and needn't reach their ends.
Inputs may be any that keep to these rules, and one draw needn't show every extreme that they name: `img_labels`: each pair id appears once among images and once among texts, so every image has exactly one matching text. `txt_labels`: each pair id appears once among texts.
All inputs are finite; a program needn't handle non-finite values.
Results may differ from the reference program's by a relative error of at most 0.024.
Values may be sent and summed in bfloat16 or wider, within the bound.
No kernel may reach another device: no remote copies, remote signals or barrier semaphores. Data moves between devices by JAX's collectives and lax.ppermute only.
A program may use at most 128 MiB of HBM per device.

```python
import math
import jax
import jax.numpy as jnp
from jax import lax

D = 1152
E = 1152
PAIRS = 16384


def steps_of(own_key, shape, shards, low, largest):
    level = 1.0
    for position, blocks in shards:
        steps = jax.random.uniform(jax.random.fold_in(jax.random.fold_in(own_key, 6), position), (blocks,), jnp.float32, low / len(shards), largest / len(shards))
        level = level * jnp.repeat(jnp.exp(steps), shape[position] // blocks).reshape((-1,) + (1,) * (len(shape) - 1 - position))
    return level


def normal_values(stream_key, dims, deviation, reach, shards=(), kind=jnp.bfloat16):
    drawn = jax.random.normal(stream_key, dims, jnp.float32) * deviation
    if len(shards) > 0:
        drawn = steps_of(stream_key, dims, shards, -0.22, 0.18) * drawn
    return jnp.clip(drawn, min=-reach, max=reach).astype(kind)


def setup_inputs(seed: int = 0) -> dict:
    key_of = jax.random.split(jax.random.key(seed), 16)
    img_hidden = normal_values(key_of[0], (PAIRS, D), 1.0, 6.0, ((0, 256),))
    txt_hidden = normal_values(key_of[1], (PAIRS, D), 1.0, 6.0, ((0, 256),))
    img_labels = jax.random.permutation(key_of[2], PAIRS).astype(jnp.int32)
    txt_labels = jax.random.permutation(key_of[3], PAIRS).astype(jnp.int32)
    img_gain = jnp.clip(1.0 + 0.18 * jax.random.normal(key_of[4], (D,), jnp.float32), 0.1, 1.9)
    img_shift = normal_values(key_of[5], (D,), 0.5, 3.0, (), jnp.float32)
    txt_gain = jnp.clip(1.0 + 0.18 * jax.random.normal(key_of[6], (D,), jnp.float32), 0.1, 1.9)
    txt_shift = normal_values(key_of[7], (D,), 0.5, 3.0, (), jnp.float32)
    img_weight = normal_values(key_of[8], (D, E), D ** -0.5, 0.1875)
    txt_weight = normal_values(key_of[9], (D, E), D ** -0.5, 0.1875)
    logit_scale = jnp.clip(jnp.exp(jax.random.uniform(key_of[10], (1,), jnp.float32, math.log(90.0), math.log(110.0))), 90.0, 110.0)
    logit_bias = jnp.clip(jax.random.uniform(key_of[11], (1,), jnp.float32, -10.5, -9.5), -10.5, -9.5)
    loss_scale = jnp.clip(jnp.exp(jax.random.uniform(key_of[12], (1,), jnp.float32, math.log(16.0), math.log(64.0))), 16.0, 64.0)
    row_moment = jnp.clip(jnp.exp(math.log(1000000000) - 4.6051702 * jax.random.uniform(key_of[13], (2, D), jnp.float32) ** steps_of(key_of[13], (2, D), ((1, 8),), -0.2, 0.2)), 10000000, 1000000000)
    col_moment = jnp.clip(jnp.exp(jax.random.uniform(key_of[14], (2, E), jnp.float32, math.log(10000000), math.log(1000000000))), 10000000, 1000000000)
    return {"img_hidden": img_hidden, "txt_hidden": txt_hidden, "img_labels": img_labels, "txt_labels": txt_labels, "img_gain": img_gain, "img_shift": img_shift, "txt_gain": txt_gain, "txt_shift": txt_shift, "img_weight": img_weight, "txt_weight": txt_weight, "logit_scale": logit_scale, "logit_bias": logit_bias, "loss_scale": loss_scale, "row_moment": row_moment, "col_moment": col_moment}


norm_eps = 1e-06
second_decay = 0.6

def head_forward(hidden, gain, shift, weight):
    values = hidden.astype(jnp.float32)
    center = lax.optimization_barrier(jnp.mean(values, axis=-1, keepdims=True))
    spread = lax.optimization_barrier(jnp.mean(jnp.square(values - center), axis=-1, keepdims=True))
    inverse = lax.rsqrt(spread + norm_eps)
    scaled = (values - center) * inverse
    normed = (scaled * gain + shift).astype(jnp.bfloat16)
    embed = jnp.dot(normed, weight, preferred_element_type=jnp.float32)
    length = jnp.sqrt(lax.optimization_barrier(jnp.sum(embed * embed, axis=-1, keepdims=True)))
    return (scaled, inverse, normed, length, embed / length)

def head_backward(d_unit, scaled, inverse, length, unit, gain, weight):
    along = lax.optimization_barrier(jnp.sum(unit * d_unit, axis=-1, keepdims=True))
    head_grad = ((d_unit - unit * along) / length).astype(jnp.bfloat16)
    d_normed = lax.dot_general(head_grad, weight, (((1,), (1,)), ((), ())), preferred_element_type=jnp.float32)
    weighted = d_normed * gain
    first = lax.optimization_barrier(jnp.mean(weighted, axis=-1, keepdims=True))
    second = lax.optimization_barrier(jnp.mean(weighted * scaled, axis=-1, keepdims=True))
    return (head_grad, (inverse * (weighted - first - scaled * second)).astype(jnp.bfloat16))

def pair_grads(img_unit, img_labels, txt_unit, txt_labels, scale, offset, factor):
    logits = scale * lax.dot_general(img_unit, txt_unit, (((1,), (1,)), ((), ())), preferred_element_type=jnp.float32) + offset
    sign = jnp.where(img_labels[:, None] == txt_labels[None, :], 1.0, -1.0).astype(logits.dtype)
    return (-(factor * scale) * sign * jax.nn.sigmoid(-sign * logits)).astype(jnp.bfloat16)

def reference(img_hidden, txt_hidden, img_labels, txt_labels, img_gain, img_shift, txt_gain, txt_shift, img_weight, txt_weight, logit_scale, logit_bias, loss_scale, row_moment, col_moment):
    img_parts = head_forward(img_hidden, img_gain, img_shift, img_weight)
    txt_parts = head_forward(txt_hidden, txt_gain, txt_shift, txt_weight)
    img_unit = img_parts[4].astype(jnp.bfloat16)
    txt_unit = txt_parts[4].astype(jnp.bfloat16)
    scale = logit_scale[0]
    offset = logit_bias[0]
    factor = loss_scale[0]
    width = img_weight.shape[1]
    blocking = math.gcd(PAIRS, 512)
    unit_blocks = img_unit.reshape(PAIRS // blocking, blocking, width)
    label_blocks = img_labels.reshape(PAIRS // blocking, blocking)

    def scan_step(text_total, item):
        units, labels = item
        pair = pair_grads(units, labels, txt_unit, txt_labels, scale, offset, factor)
        image_part = jnp.dot(pair, txt_unit, preferred_element_type=jnp.float32)
        text_total = text_total + lax.dot_general(pair, units, (((0,), (0,)), ((), ())), preferred_element_type=jnp.float32)
        return (text_total, image_part)
    start_total = jnp.zeros((PAIRS, width), jnp.float32)
    txt_dunit, image_blocks = lax.scan(scan_step, start_total, (unit_blocks, label_blocks))
    img_dunit = image_blocks.reshape(PAIRS, width)
    img_head, img_grad = head_backward(img_dunit, img_parts[0], img_parts[1], img_parts[3], img_parts[4], img_gain, img_weight)
    txt_head, txt_grad = head_backward(txt_dunit, txt_parts[0], txt_parts[1], txt_parts[3], txt_parts[4], txt_gain, txt_weight)
    grad_image = lax.dot_general(img_parts[2], img_head, (((0,), (0,)), ((), ())), preferred_element_type=jnp.float32)
    grad_text = lax.dot_general(txt_parts[2], txt_head, (((0,), (0,)), ((), ())), preferred_element_type=jnp.float32)
    grads = jnp.concatenate([grad_image, grad_text], axis=1)
    depth = grads.shape[0]
    squares = (grads * grads).reshape(depth, 2, width)
    row_new = second_decay * row_moment + (1.0 - second_decay) * lax.optimization_barrier(jnp.mean(squares, axis=2)).T
    col_new = second_decay * col_moment + (1.0 - second_decay) * lax.optimization_barrier(jnp.mean(squares, axis=0))
    row_mean = lax.optimization_barrier(jnp.mean(row_new, axis=1))
    denom = jnp.sqrt(row_new.T[:, :, None] * col_new[None, :, :] / row_mean[None, :, None])
    update = (grads.reshape(depth, 2, width) / denom).reshape(depth, 2 * width)
    return (img_grad, txt_grad, update, row_new, col_new)
```

```python
import itertools

import jax
import jax.numpy as jnp
from jax import lax
from jax.sharding import Mesh
from jax.sharding import PartitionSpec as P

norm_eps = 1e-06
second_decay = 0.6
label_base = 128
sizes = {"z": 8, "h": 2, "c": 2, "l": 2, "x": 4}
every = ("z", "h", "c", "l", "x")
rows_spec = P(every)
txt_axes = ("l", "x")


def route(axes, move):
    spots = list(itertools.product(*[range(sizes[a]) for a in axes]))
    index = {spot: i for i, spot in enumerate(spots)}
    pairs = []
    for spot in spots:
        there = move(dict(zip(axes, spot)))
        pairs.append((index[spot], index[tuple(there[a] % sizes[a] for a in axes)]))
    return pairs


def send(block, axes, move):
    return lax.ppermute(block, axes, route(axes, move))


def along(axis, by):
    return lambda at: {axis: at[axis] + by}


def turn_y(at, by):
    y = (at["h"] * 2 + at["l"] + by) % 4
    return {**at, "h": y // 2, "l": y % 2}


def turn_x(at, by):
    return {**at, "x": at["x"] + by}


plane = ("h", "c", "l", "x")


def plane_first(by):
    return lambda at: turn_x(at, by) if at["c"] == 0 else turn_y(at, by)


def plane_second(by):
    return lambda at: turn_y(at, by) if at["c"] == 0 else turn_x(at, by)


def swap_core(block):
    return send(block, ("c",), along("c", 1))


def head_forward(hidden, gain, shift, weight):
    values = hidden.astype(jnp.float32)
    center = jnp.mean(values, axis=-1, keepdims=True)
    spread = jnp.mean(jnp.square(values - center), axis=-1, keepdims=True)
    inverse = lax.rsqrt(spread + norm_eps)
    scaled = (values - center) * inverse
    normed = (scaled * gain + shift).astype(jnp.bfloat16)
    embed = jnp.dot(normed, weight, preferred_element_type=jnp.float32)
    length = jnp.sqrt(jnp.sum(embed * embed, axis=-1, keepdims=True))
    return (scaled, inverse, normed, length, embed / length)


def head_backward(d_unit, scaled, inverse, length, unit, gain, weight):
    projected = jnp.sum(unit * d_unit, axis=-1, keepdims=True)
    head_grad = ((d_unit - unit * projected) / length).astype(jnp.bfloat16)
    d_normed = lax.dot_general(
        head_grad, weight, (((1,), (1,)), ((), ())), preferred_element_type=jnp.float32
    )
    weighted = d_normed * gain
    first = jnp.mean(weighted, axis=-1, keepdims=True)
    second = jnp.mean(weighted * scaled, axis=-1, keepdims=True)
    return (head_grad, (inverse * (weighted - first - scaled * second)).astype(jnp.bfloat16))


def with_labels(unit, labels):
    rows, width = unit.shape
    digits = jnp.concatenate([labels // label_base, labels % label_base]).astype(jnp.bfloat16)
    below = jnp.pad(digits[None, :], ((0, 7), (0, width - 2 * rows)))
    return jnp.concatenate([unit.astype(jnp.bfloat16), below], axis=0)


def split_labels(blocks, rows):
    count, _, width = blocks.shape
    units = blocks[:, :rows].reshape(count * rows, width)
    digits = blocks[:, rows, : 2 * rows].astype(jnp.int32)
    labels = digits[:, :rows] * label_base + digits[:, rows:]
    return units, labels.reshape(count * rows)


def gather_plane(block):
    near = jnp.stack([block] + [send(block, plane, plane_first(k)) for k in (1, 2, 3)])
    return jnp.stack([near] + [send(near, plane, plane_second(k)) for k in (1, 2, 3)])


def scatter_plane(parts):
    near = parts[0].astype(jnp.float32)
    for j in (1, 2, 3):
        near = near + send(parts[j], plane, plane_second(-j)).astype(jnp.float32)
    own = near[0]
    for k in (1, 2, 3):
        own = own + send(near[k].astype(jnp.bfloat16), plane, plane_first(-k)).astype(jnp.float32)
    return own


def gather_column(block):
    half = 32
    up, down = block, block
    below, above = [], []
    for _ in range(3):
        up = send(up, ("z",), along("z", 1))
        down = send(down, ("z",), along("z", -1))
        below.append(up)
        above.append(down)
    far = jnp.concatenate(
        [
            send(up[:half], ("z",), along("z", 1)),
            send(down[half:], ("z",), along("z", -1)),
        ]
    )
    mine = jnp.stack([block] + below + above + [far])
    return jnp.concatenate([mine, swap_core(mine)])


def scatter_column(parts):
    half = 32
    mine = parts[:8].astype(jnp.float32) + swap_core(parts[8:]).astype(jnp.float32)
    far = mine[7].astype(jnp.bfloat16)
    low = send(far[:half], ("z",), along("z", -1)).astype(jnp.float32)
    high = send(far[half:], ("z",), along("z", 1)).astype(jnp.float32)
    rest = mine.shape[1] - half
    low = jnp.pad(low, ((0, rest), (0, 0)))
    high = jnp.pad(high, ((half, 0), (0, 0)))
    for step in (3, 2, 1):
        low = (mine[step] + low).astype(jnp.bfloat16)
        high = (mine[3 + step] + high).astype(jnp.bfloat16)
        low = send(low, ("z",), along("z", -1)).astype(jnp.float32)
        high = send(high, ("z",), along("z", 1)).astype(jnp.float32)
    return mine[0] + low + high


def pair_grads(img_unit, img_labels, txt_unit, txt_labels, scale, offset, factor):
    logits = (
        scale
        * lax.dot_general(
            img_unit, txt_unit, (((1,), (1,)), ((), ())), preferred_element_type=jnp.float32
        )
        + offset
    )
    match = img_labels[:, None] == txt_labels[None, :]
    ratio = 1.0 / (1.0 + jnp.exp(jnp.where(match, logits, -logits)))
    size = factor * scale
    return (jnp.where(match, -size, size) * ratio).astype(jnp.bfloat16)


def shards(
    img_hidden,
    txt_hidden,
    img_labels,
    txt_labels,
    img_gain,
    img_shift,
    txt_gain,
    txt_shift,
    img_weight,
    txt_weight,
    logit_scale,
    logit_bias,
    loss_scale,
    row_moment,
    col_moment,
):
    rows, width = img_hidden.shape
    depth = img_weight.shape[0]
    core = lax.axis_index("c")
    x_at = lax.axis_index("x")
    y_at = lax.axis_index("h") * 2 + lax.axis_index("l")

    img_parts = head_forward(img_hidden, img_gain, img_shift, img_weight)
    txt_parts = head_forward(txt_hidden, txt_gain, txt_shift, txt_weight)
    img_blocks = gather_plane(with_labels(img_parts[4], img_labels))
    txt_blocks = gather_column(with_labels(txt_parts[4], txt_labels))
    img_units, img_ids = split_labels(img_blocks.reshape(16, -1, width), rows)
    txt_units, txt_ids = split_labels(txt_blocks, rows)

    first = core == 0
    img_normed, txt_normed = img_parts[2], txt_parts[2]
    normed = jnp.concatenate(
        [
            jnp.where(first, img_normed, txt_normed),
            swap_core(jnp.where(first, txt_normed, img_normed)),
        ]
    )
    split_normed = normed.T.reshape(2, 4, depth // 8, 2 * rows)

    def rows_of(by):
        return lax.dynamic_index_in_dim(split_normed, (x_at + by) % 4, 1, keepdims=False)

    normed_cols = jnp.concatenate(
        [rows_of(0)] + [send(rows_of(k), ("x",), along("x", k)) for k in (1, 2, 3)], axis=-1
    ).reshape(depth // 4, 8 * rows)

    pair = pair_grads(
        img_units, img_ids, txt_units, txt_ids, logit_scale[0], logit_bias[0], loss_scale[0]
    )
    img_sums = jnp.dot(pair, txt_units, preferred_element_type=jnp.float32).astype(jnp.bfloat16)
    txt_sums = lax.dot_general(
        pair, img_units, (((0,), (0,)), ((), ())), preferred_element_type=jnp.float32
    ).astype(jnp.bfloat16)
    img_dunit = scatter_plane(img_sums.reshape(4, 4, rows, width))
    txt_dunit = scatter_column(txt_sums.reshape(16, rows, width))

    img_head, img_grad = head_backward(
        img_dunit, img_parts[0], img_parts[1], img_parts[3], img_parts[4], img_gain, img_weight
    )
    txt_head, txt_grad = head_backward(
        txt_dunit, txt_parts[0], txt_parts[1], txt_parts[3], txt_parts[4], txt_gain, txt_weight
    )
    head = jnp.concatenate(
        [
            jnp.where(first, img_head, txt_head),
            swap_core(jnp.where(first, txt_head, img_head)),
        ]
    )
    heads = jnp.concatenate([head] + [send(head, ("x",), along("x", k)) for k in (1, 2, 3)])
    partial = jnp.dot(normed_cols, heads, preferred_element_type=jnp.float32).astype(jnp.bfloat16)
    partial = partial.reshape(2, 2, 8, depth // 128, width)

    def piece_of(by):
        y = (y_at + by) % 4
        return lax.dynamic_slice(
            partial, (y % 2, y // 2, 0, 0, 0), (1, 1) + partial.shape[2:]
        )[0, 0]

    total = piece_of(0).astype(jnp.float32)
    for k in (1, 2, 3):
        total = total + send(piece_of(k), ("h", "l"), lambda at: turn_y(at, k)).astype(jnp.float32)
    total = lax.all_to_all(total.astype(jnp.bfloat16), "z", 0, 0, tiled=True)
    total = jnp.sum(total.astype(jnp.float32), axis=0).astype(jnp.bfloat16)
    total = lax.all_to_all(
        jnp.broadcast_to(total[None], (8,) + total.shape), "z", 0, 0, tiled=True
    ).reshape(depth // 16, width)
    other = send(total, ("h",), along("h", 1))
    low = lax.axis_index("h") == 0
    total = jnp.concatenate([jnp.where(low, total, other), jnp.where(low, other, total)])
    other = swap_core(total)
    grads = jnp.stack([jnp.where(first, total, other), jnp.where(first, other, total)], axis=1)
    grads = grads.astype(jnp.float32)

    squares = grads * grads
    row_new = second_decay * row_moment + (1.0 - second_decay) * jnp.mean(squares, axis=2).T
    col_total, row_total = lax.psum((jnp.sum(squares, axis=0), jnp.sum(row_new, axis=1)), txt_axes)
    col_new = second_decay * col_moment + (1.0 - second_decay) * (col_total / depth)
    row_mean = row_total / depth
    denom = jnp.sqrt(row_new.T[:, :, None] * col_new[None, :, :] / row_mean[None, :, None])
    update = (grads / denom).reshape(depth // 8, 2 * width)
    return (img_grad, txt_grad, update, row_new, col_new)


def solution(mesh):
    fine = Mesh(mesh.devices.reshape([sizes[a] for a in every]), every)
    whole = P()
    in_specs = (rows_spec,) * 4 + (whole,) * 9 + (P(None, txt_axes), whole)
    out_specs = (rows_spec, rows_spec, P(txt_axes), P(None, txt_axes), whole)
    return jax.shard_map(shards, mesh=fine, in_specs=in_specs, out_specs=out_specs, check_vma=False)
```

```python
import functools
import itertools

import jax
import jax.numpy as jnp
from jax import lax
from jax.experimental import pallas as pl
from jax.experimental.pallas import tpu as pltpu
from jax.sharding import Mesh
from jax.sharding import PartitionSpec as P

norm_eps = 1e-06
second_decay = 0.6
label_base = 128
piece_rows = 16
sizes = {"z": 8, "h": 2, "c": 2, "l": 2, "x": 4}
every = ("z", "h", "c", "l", "x")
rows_spec = P(every)
txt_axes = ("l", "x")


def route(axes, move):
    spots = list(itertools.product(*[range(sizes[a]) for a in axes]))
    index = {spot: i for i, spot in enumerate(spots)}
    pairs = []
    for spot in spots:
        there = move(dict(zip(axes, spot)))
        pairs.append((index[spot], index[tuple(there[a] % sizes[a] for a in axes)]))
    return pairs


def send(block, axes, move):
    return lax.ppermute(block, axes, route(axes, move))


def along(axis, by):
    return lambda at: {axis: at[axis] + by}


def turn_y(at, by):
    y = (at["h"] * 2 + at["l"] + by) % 4
    return {**at, "h": y // 2, "l": y % 2}


def turn_x(at, by):
    return {**at, "x": at["x"] + by}


plane = ("h", "c", "l", "x")


def plane_first(by):
    return lambda at: turn_x(at, by) if at["c"] == 0 else turn_y(at, by)


def plane_second(by):
    return lambda at: turn_y(at, by) if at["c"] == 0 else turn_x(at, by)


def swap_core(block):
    return send(block, ("c",), along("c", 1))


def forward_kernel(at, hidden, gain, shift, labels, weight, *refs):
    rows, width = hidden.shape
    block, scaled, kept, normed_outs = refs[-5], refs[-4], refs[-3], refs[-2:]
    values = hidden[...].astype(jnp.float32)
    center = jnp.mean(values, axis=-1, keepdims=True)
    spread = jnp.mean(jnp.square(values - center), axis=-1, keepdims=True)
    inverse = lax.rsqrt(spread + norm_eps)
    scaled[...] = (values - center) * inverse
    normed = (scaled[...] * gain[...] + shift[...]).astype(jnp.bfloat16)
    embed = jnp.dot(normed, weight[...], preferred_element_type=jnp.float32)
    length = jnp.sqrt(jnp.sum(embed * embed, axis=-1, keepdims=True))
    unit = embed / length
    kept[:, :width] = unit
    lane = lax.broadcasted_iota(jnp.int32, (rows, label_base), 1)
    kept[:, width:] = jnp.where(lane == 0, length, inverse)
    block[:, :width] = unit.astype(jnp.bfloat16)
    one, two = (lax.broadcasted_iota(jnp.int32, (rows, rows), d) for d in (0, 1))
    column = jnp.where(one == two, labels[...], 0).astype(jnp.float32)
    column = jnp.sum(column, axis=1, keepdims=True).astype(jnp.int32)
    digits = jnp.where(lane == 0, column // label_base, column % label_base)
    digits = jnp.where(lane < 2, digits, 0).astype(jnp.float32)
    block[:, width:] = digits.astype(jnp.bfloat16)
    if len(refs) == 5:
        normed_outs[0][...] = normed
        normed_outs[1][...] = normed
    else:
        keep_or_give(at[0], normed, refs[0][...], *normed_outs)


def keep_or_give(first, image, text, keep, give):
    keep[...] = jnp.where(first == 1, image, text)
    give[...] = jnp.where(first == 1, text, image)


def head_forward(at, hidden, labels, gain, shift, weight, text_normed=()):
    rows, width = hidden.shape
    vmem = pl.BlockSpec(memory_space=pltpu.VMEM)
    smem = pl.BlockSpec(memory_space=pltpu.SMEM)
    shape = jax.ShapeDtypeStruct
    wide = weight.shape[1] + label_base
    return pl.pallas_call(
        forward_kernel,
        out_shape=[
            shape((rows, wide), jnp.bfloat16),
            shape((rows, width), jnp.float32),
            shape((rows, wide), jnp.float32),
            shape((rows, width), jnp.bfloat16),
            shape((rows, width), jnp.bfloat16),
        ],
        in_specs=[smem] + [vmem] * (5 + len(text_normed)),
        out_specs=[vmem, pl.BlockSpec(), pl.BlockSpec(), vmem, vmem],
        compiler_params=pltpu.CompilerParams(vmem_limit_bytes=8 * 1024 * 1024),
    )(at, hidden, gain[None, :], shift[None, :], labels[None, :], weight, *text_normed)


def heads_kernel(count, at, img_kept, txt_kept, *refs):
    heads, keep, give = refs[-4:-2], refs[-2], refs[-1]
    for kept, terms, head in (
        (img_kept, refs[:count], heads[0]),
        (txt_kept, refs[count:-4], heads[1]),
    ):
        rows, width = head.shape
        unit, length = kept[:, :width], kept[:, width : width + 1]
        d_unit = sum(ref[:rows, :width].astype(jnp.float32) for ref in terms)
        projected = jnp.sum(unit * d_unit, axis=-1, keepdims=True)
        head[...] = ((d_unit - unit * projected) / length).astype(jnp.bfloat16)
    keep_or_give(at[0], heads[0][...], heads[1][...], keep, give)


def head_gradients(at, img_kept, txt_kept, img_terms, txt_terms):
    rows, width = img_kept.shape[0], img_kept.shape[1] - label_base
    vmem = pl.BlockSpec(memory_space=pltpu.VMEM)
    smem = pl.BlockSpec(memory_space=pltpu.SMEM)
    return pl.pallas_call(
        functools.partial(heads_kernel, len(img_terms)),
        out_shape=[jax.ShapeDtypeStruct((rows, width), jnp.bfloat16)] * 4,
        in_specs=[smem] + [vmem] * (2 + len(img_terms) + len(txt_terms)),
        out_specs=[vmem] * 4,
        compiler_params=pltpu.CompilerParams(vmem_limit_bytes=4 * 1024 * 1024),
    )(at, img_kept, txt_kept, *img_terms, *txt_terms)


def backward_kernel(head_grad, scaled, kept, gain, weight, out):
    width = scaled.shape[1]
    inverse = kept[:, width + 1 : width + 2]
    d_normed = lax.dot_general(
        head_grad[...],
        weight[...],
        (((1,), (1,)), ((), ())),
        preferred_element_type=jnp.float32,
    )
    weighted = d_normed * gain[...]
    first = jnp.mean(weighted, axis=-1, keepdims=True)
    second = jnp.mean(weighted * scaled[...], axis=-1, keepdims=True)
    out[...] = (inverse * (weighted - first - scaled[...] * second)).astype(jnp.bfloat16)


def norm_backward(head_grad, scaled, kept, gain, weight):
    return pl.pallas_call(
        backward_kernel,
        out_shape=jax.ShapeDtypeStruct(scaled.shape, jnp.bfloat16),
        compiler_params=pltpu.CompilerParams(vmem_limit_bytes=8 * 1024 * 1024),
        cost_estimate=pl.CostEstimate(
            flops=2 * scaled.size * weight.shape[0], bytes_accessed=8 * 2**20, transcendentals=0
        ),
    )(head_grad, scaled, kept, gain[None, :], weight)


def weight_kernel(at, *refs):
    heads, normed, outs = refs[:4], refs[4:8], refs[8:]
    lanes = 8 * 128
    for out, by in zip(outs, (0, 1, 3, 2)):
        start = (at[2] + by) % 4 * 256
        total = None
        for head, piece in zip(heads, normed):
            from_lane = pl.multiple_of(start + piece.shape[1] - lanes, 128)
            rows = piece[:, pl.ds(from_lane, 256)]
            rows = jnp.concatenate([rows[:, :128], rows[:, 128:]], axis=0)
            term = jnp.dot(rows, head[...], preferred_element_type=jnp.float32)
            total = term if total is None else total + term
        out[...] = total.astype(jnp.bfloat16)


def weight_parts(at, heads, normed):
    width = heads[0].shape[1]
    vmem = pl.BlockSpec(memory_space=pltpu.VMEM)
    return pl.pallas_call(
        weight_kernel,
        out_shape=[jax.ShapeDtypeStruct((8 * piece_rows, width), jnp.bfloat16)] * 4,
        in_specs=[pl.BlockSpec(memory_space=pltpu.SMEM)] + [vmem] * 8,
        out_specs=[vmem] * 4,
        compiler_params=pltpu.CompilerParams(vmem_limit_bytes=4 * 1024 * 1024),
    )(at, *heads, *normed)


def pick_kernel(at, keep, got, *outs):
    first, at_first, z_at = at[0], at[1], at[3]
    width = keep.shape[1]
    short = width // 128
    normed = jnp.concatenate([keep[...], got[...]], axis=0)
    spot = lax.broadcasted_iota(jnp.int32, (8 * piece_rows, 1), 0)
    column = lax.broadcasted_iota(jnp.int32, (8 * piece_rows, width), 1)
    slot = spot // piece_rows
    inner = (slot ^ z_at) * short + spot % piece_rows
    for by, out in enumerate(outs):
        one = (at_first + by) % 4
        for two in range(4):
            by_x = two % 2 * 8 + one * 2 + two // 2
            by_y = one % 2 * 8 + two * 2 + one // 2
            row = jnp.where(first == 1, by_x, by_y) * (8 * short) + inner
            row = jnp.where(spot % piece_rows < short, row, -1)
            chosen = jnp.where(column == row, 1.0, 0.0).astype(jnp.bfloat16)
            picked = lax.dot_general(
                chosen, normed, (((1,), (1,)), ((), ())), preferred_element_type=jnp.float32
            ).astype(jnp.bfloat16)
            out[:, 256 * two : 256 * two + 128] = picked[:64, :]
            out[:, 256 * two + 128 : 256 * (two + 1)] = picked[64:, :]


def order_kernel(at, *refs):
    z_at, h_at = at[3], at[4]
    rows, width = refs[-1].shape
    short = rows // 16
    total = None
    for k, ref in enumerate(refs[:-1]):
        spot = lax.broadcasted_iota(jnp.int32, (rows, 4 * piece_rows), 1)
        row = (z_at ^ 2 * k ^ spot // piece_rows % 2) * short + spot % piece_rows
        row = row + (h_at ^ spot // (2 * piece_rows)) * (8 * short)
        row = jnp.where(spot % piece_rows < short, row, -1)
        chosen = lax.broadcasted_iota(jnp.int32, (rows, 4 * piece_rows), 0) == row
        chosen = jnp.where(chosen, 1.0, 0.0).astype(jnp.bfloat16)
        term = jnp.dot(chosen, ref[...], preferred_element_type=jnp.float32)
        total = term if total is None else total + term
    refs[-1][...] = total.astype(jnp.bfloat16)


def order_rows(at, slots, rows):
    vmem = pl.BlockSpec(memory_space=pltpu.VMEM)
    return pl.pallas_call(
        order_kernel,
        out_shape=jax.ShapeDtypeStruct((rows, slots[0].shape[1]), jnp.bfloat16),
        in_specs=[pl.BlockSpec(memory_space=pltpu.SMEM)] + [vmem] * 4,
        out_specs=vmem,
        compiler_params=pltpu.CompilerParams(vmem_limit_bytes=3 * 1024 * 1024),
    )(at, *slots)


def hop(block, z_by, h_by=0):
    return send(block, ("z", "h"), lambda at: {"z": at["z"] ^ z_by, "h": at["h"] ^ h_by})


def tie(*arrays):
    return lax.optimization_barrier(arrays)


def gather_units(txt_block, img_block, give_normed):
    up, down = send_z(txt_block, 1), send_z(txt_block, -1)
    up, down, img_block = tie(up, down, img_block)
    mine = [txt_block, up, down]
    up, down = send_z(up, 1), send_z(down, -1)
    near = [img_block] + [send(img_block, plane, plane_first(k)) for k in (1, 3, 2)]
    up, down, near = tie(up, down, jnp.concatenate(near))
    mine = [jnp.concatenate(mine + [up, down])]
    up, down = send_z(up, 1), send_z(down, -1)
    images = [near] + [send(near, plane, plane_second(k)) for k in (1, 2, 3)]
    other = [swap_core(mine[0])]
    got_normed = swap_core(give_normed)
    up, down, got_normed = tie(up, down, got_normed)
    mine.append(jnp.concatenate([up, down, send_z(up, 1)]))
    other.append(swap_core(mine[1]))
    return images, mine, other, got_normed


def scatter_units(img_parts, txt_mine, txt_other, pieces):
    rows = txt_mine.shape[0] // 8
    f32, bf16 = jnp.float32, jnp.bfloat16
    swapped, *img_parts = tie(swap_core(txt_other), *img_parts)
    away = [send(img_parts[k], plane, plane_second(-k)) for k in (1, 3, 2)]

    def part(i):
        at = slice(rows * i, rows * (i + 1))
        return txt_mine[at].astype(f32) + swapped[at].astype(f32)

    def onward(i, arrived):
        return (part(i) + arrived.astype(f32)).astype(bf16)

    low, one = tie(send_z(part(7).astype(bf16), -1), away[0])
    low, high = onward(5, low), part(6).astype(bf16)
    low, high = send_z(low, -1), send_z(high, 1)
    low, high, three = tie(low, high, away[1])
    low, high = onward(3, low), onward(4, high)
    low, high = send_z(low, -1), send_z(high, 1)
    low, high, two = tie(low, high, away[2])
    low, high = onward(1, low), onward(2, high)
    low, high = send_z(low, -1), send_z(high, 1)
    away = [one, three, two]
    near = img_parts[0].astype(f32) + sum(block.astype(f32) for block in away)
    img_terms = [near[:rows]]
    for i, k in enumerate((1, 3, 2)):
        block = near[rows * (i + 1) : rows * (i + 2)].astype(bf16)
        block = jnp.concatenate([block, pieces[(4 - k) % 4]], axis=1)
        img_terms.append(send(block, plane, plane_first(-k)))
    return img_terms, [txt_mine, swapped, low, high]


def send_z(block, by):
    return send(block, ("z",), along("z", by))


def pair_kernel(consts, *refs):
    images, texts = refs[:4], refs[4:8]
    pair_ref, all_ref, mine_ref, other_ref, digits, total = refs[8:]
    width = all_ref.shape[1]
    step = images[0].shape[0]
    scale, offset, size = consts[0], consts[1], consts[2]
    at = 0
    for ref in texts:
        rows = ref.shape[0]
        all_ref[at : at + rows, :] = ref[:, :width]
        digits[at : at + rows, :] = ref[:, width:].astype(jnp.float32)
        at += rows
    for q in range(4):
        here = slice(step * q, step * (q + 1))
        text = all_ref[here, :]
        turned = digits[here, :].T
        txt_ids = turned[0:1, :] * label_base + turned[1:2, :]
        for j in range(4):
            image = images[j][:, :width]
            below = images[j][:, width:].astype(jnp.float32)
            img_ids = below[:, 0:1] * label_base + below[:, 1:2]
            dots = lax.dot_general(
                image, text, (((1,), (1,)), ((), ())), preferred_element_type=jnp.float32
            )
            logits = dots * scale + offset
            match = img_ids == txt_ids
            ratio = 1.0 / (1.0 + jnp.exp(jnp.where(match, logits, -logits)))
            pair = (jnp.where(match, -size, size) * ratio).astype(jnp.bfloat16)
            pair_ref[step * j : step * (j + 1), here] = pair
            part = lax.dot_general(
                pair, image, (((0,), (0,)), ((), ())), preferred_element_type=jnp.float32
            )
            if j == 0:
                total[...] = part
            else:
                total[...] += part
        out_ref = (mine_ref, other_ref)[q // 2]
        out_ref[step * (q % 2) : step * (q % 2 + 1), :] = total[...].astype(jnp.bfloat16)


def image_kernel(at, pair_ref, all_ref, keep, got, *outs):
    step = outs[0].shape[0]
    for j in range(4):
        outs[j][...] = jnp.dot(
            pair_ref[step * j : step * (j + 1), :],
            all_ref[...],
            preferred_element_type=jnp.float32,
        ).astype(jnp.bfloat16)
    pick_kernel(at, keep, got, *outs[4:])


def pair_products(images, mine, other, consts, at, keep, got):
    rows, width = keep.shape
    step = images[0].shape[0]
    count = 4 * step
    vmem = pl.BlockSpec(memory_space=pltpu.VMEM)
    params = pltpu.CompilerParams(vmem_limit_bytes=6 * 1024 * 1024)
    shape = functools.partial(jax.ShapeDtypeStruct, dtype=jnp.bfloat16)
    pair, texts, txt_mine, txt_other = pl.pallas_call(
        pair_kernel,
        out_shape=[
            shape((count, count)),
            shape((count, width)),
            shape((count // 2, width)),
            shape((count // 2, width)),
        ],
        in_specs=[pl.BlockSpec(memory_space=pltpu.SMEM)] + [vmem] * 8,
        out_specs=[vmem] * 4,
        scratch_shapes=[
            pltpu.VMEM((count, label_base), jnp.float32),
            pltpu.VMEM((step, width), jnp.float32),
        ],
        compiler_params=params,
        cost_estimate=pl.CostEstimate(
            flops=4 * count * count * width, bytes_accessed=12 * 2**20, transcendentals=2 * count**2
        ),
    )(consts, *images, *mine, *other)
    parts = pl.pallas_call(
        image_kernel,
        out_shape=[shape((step, width))] * 4 + [shape((rows, 8 * 128))] * 4,
        in_specs=[pl.BlockSpec(memory_space=pltpu.SMEM)] + [vmem] * 4,
        out_specs=[vmem] * 8,
        compiler_params=pltpu.CompilerParams(vmem_limit_bytes=8 * 1024 * 1024),
        cost_estimate=pl.CostEstimate(
            flops=2 * count * count * width, bytes_accessed=8 * 2**20, transcendentals=0
        ),
    )(at, pair, texts, keep, got)
    return parts[:4], parts[4:], txt_mine, txt_other


def shards(
    img_hidden,
    txt_hidden,
    img_labels,
    txt_labels,
    img_gain,
    img_shift,
    txt_gain,
    txt_shift,
    img_weight,
    txt_weight,
    logit_scale,
    logit_bias,
    loss_scale,
    row_moment,
    col_moment,
):
    rows, width = img_hidden.shape
    depth = img_weight.shape[0]
    first = lax.axis_index("c") == 0
    x_at = lax.axis_index("x")
    y_at = lax.axis_index("h") * 2 + lax.axis_index("l")
    at = [
        1 - lax.axis_index("c"),
        jnp.where(first, x_at, y_at),
        jnp.where(first, y_at, x_at),
        lax.axis_index("z"),
        lax.axis_index("h"),
    ]
    consts = [logit_scale[0], logit_bias[0], loss_scale[0] * logit_scale[0]]
    at, consts, txt_hidden = tie(jnp.stack(at), jnp.stack(consts), txt_hidden)

    txt_block, txt_scaled, txt_kept, txt_normed, _ = head_forward(
        at, txt_hidden, txt_labels, txt_gain, txt_shift, txt_weight
    )
    txt_block, img_hidden = tie(txt_block, img_hidden)
    img_block, img_scaled, img_kept, keep_normed, give_normed = head_forward(
        at, img_hidden, img_labels, img_gain, img_shift, img_weight, (txt_normed,)
    )
    images, mine, other, got_normed = gather_units(txt_block, img_block, give_normed)
    img_parts, pieces, txt_mine, txt_other = pair_products(
        images,
        mine,
        other,
        consts,
        at,
        keep_normed,
        got_normed,
    )
    img_terms, txt_terms = scatter_units(img_parts, txt_mine, txt_other, pieces)
    img_head, txt_head, keep_head, give_head = head_gradients(
        at, img_kept, txt_kept, img_terms, txt_terms
    )
    img_grad = norm_backward(img_head, img_scaled, img_kept, img_gain, img_weight)
    txt_grad = norm_backward(txt_head, txt_scaled, txt_kept, txt_gain, txt_weight)
    head = jnp.concatenate([keep_head, swap_core(give_head)])
    heads = [head] + [send(head, plane, plane_first(-k)) for k in (1, 3, 2)]
    own, *away = weight_parts(at, heads, [pieces[0]] + img_terms[1:])
    total = own.astype(jnp.float32)
    for k, block in zip((1, 3, 2), away):
        total = total + send(block, plane, plane_second(k)).astype(jnp.float32)
    total = total.astype(jnp.bfloat16)
    sent = [hop(total[32 * i : 32 * (i + 1)], 2 * i) for i in (1, 2, 3)]
    total = total[:32].astype(jnp.float32) + sum(block.astype(jnp.float32) for block in sent)
    total = total.astype(jnp.bfloat16)
    total = total[:16].astype(jnp.float32) + hop(total[16:], 1).astype(jnp.float32)
    total = total.astype(jnp.bfloat16)
    four = jnp.concatenate([total, hop(total, 1), hop(total, 0, 1), hop(total, 1, 1)])
    slots = [four] + [hop(four, k) for k in (2, 4, 6)]
    total = order_rows(at, slots, depth // 8)
    other = swap_core(total)
    towers = [jnp.where(first, total, other), jnp.where(first, other, total)]
    towers = [grads.astype(jnp.float32) for grads in towers]

    squares = [grads * grads for grads in towers]
    row_means = jnp.stack([jnp.mean(square, axis=1) for square in squares])
    row_new = second_decay * row_moment + (1.0 - second_decay) * row_means
    row_sums = jnp.pad(jnp.sum(row_new, axis=1)[:, None], ((0, 0), (0, 127)))
    col_sums = jnp.stack([jnp.sum(square, axis=0) for square in squares])
    sums = jnp.concatenate([col_sums, row_sums], axis=1)
    sums = jnp.broadcast_to(sums[None], (8,) + sums.shape)
    sums = jnp.sum(lax.all_to_all(sums, txt_axes, 0, 0, tiled=True), axis=0)
    col_new = second_decay * col_moment + (1.0 - second_decay) * (sums[:, :width] / depth)
    row_mean = sums[:, width] / depth
    update = jnp.concatenate(
        [
            towers[k] / jnp.sqrt(row_new[k][:, None] * col_new[k][None, :] / row_mean[k])
            for k in (0, 1)
        ],
        axis=1,
    )
    return (img_grad, txt_grad, update, row_new, col_new)


def solution(mesh):
    fine = Mesh(mesh.devices.reshape([sizes[a] for a in every]), every)
    whole = P()
    in_specs = (rows_spec,) * 4 + (whole,) * 9 + (P(None, txt_axes), whole)
    out_specs = (rows_spec, rows_spec, P(txt_axes), P(None, txt_axes), whole)
    return jax.shard_map(shards, mesh=fine, in_specs=in_specs, out_specs=out_specs, check_vma=False)
```

```python
import functools
import itertools

import jax
import jax.numpy as jnp
from jax import lax
from jax.experimental import pallas as pl
from jax.experimental.pallas import tpu as pltpu
from jax.sharding import Mesh
from jax.sharding import PartitionSpec as P

norm_eps = 1e-06
second_decay = 0.6
label_base = 128
piece_rows = 16
sizes = {"z": 8, "h": 2, "c": 2, "l": 2, "x": 4}
every = ("z", "h", "c", "l", "x")
rows_spec = P(every)
txt_axes = ("l", "x")


def route(axes, move):
    spots = list(itertools.product(*[range(sizes[a]) for a in axes]))
    index = {spot: i for i, spot in enumerate(spots)}
    pairs = []
    for spot in spots:
        there = move(dict(zip(axes, spot)))
        pairs.append((index[spot], index[tuple(there[a] % sizes[a] for a in axes)]))
    return pairs


def send(block, axes, move):
    return lax.ppermute(block, axes, route(axes, move))


def along(axis, by):
    return lambda at: {axis: at[axis] + by}


def turn_y(at, by):
    y = (at["h"] * 2 + at["l"] + by) % 4
    return {**at, "h": y // 2, "l": y % 2}


def turn_x(at, by):
    return {**at, "x": at["x"] + by}


plane = ("h", "c", "l", "x")


def plane_first(by):
    return lambda at: turn_x(at, by) if at["c"] == 0 else turn_y(at, by)


def plane_second(by):
    return lambda at: turn_y(at, by) if at["c"] == 0 else turn_x(at, by)


def swap_core(block):
    return send(block, ("c",), along("c", 1))


def forward_kernel(at, hidden, gain, shift, labels, weight, *refs):
    rows, width = hidden.shape
    block, scaled, kept, normed_outs = refs[-5], refs[-4], refs[-3], refs[-2:]
    values = hidden[...].astype(jnp.float32)
    center = jnp.mean(values, axis=-1, keepdims=True)
    spread = jnp.mean(jnp.square(values - center), axis=-1, keepdims=True)
    inverse = lax.rsqrt(spread + norm_eps)
    scaled[...] = (values - center) * inverse
    normed = (scaled[...] * gain[...] + shift[...]).astype(jnp.bfloat16)
    embed = jnp.dot(normed, weight[...], preferred_element_type=jnp.float32)
    length = jnp.sqrt(jnp.sum(embed * embed, axis=-1, keepdims=True))
    unit = embed / length
    kept[:, :width] = unit
    lane = lax.broadcasted_iota(jnp.int32, (rows, label_base), 1)
    kept[:, width:] = jnp.where(lane == 0, length, inverse)
    block[:, :width] = unit.astype(jnp.bfloat16)
    one, two = (lax.broadcasted_iota(jnp.int32, (rows, rows), d) for d in (0, 1))
    column = jnp.where(one == two, labels[...], 0).astype(jnp.float32)
    column = jnp.sum(column, axis=1, keepdims=True).astype(jnp.int32)
    digits = jnp.where(lane == 0, column // label_base, column % label_base)
    digits = jnp.where(lane < 2, digits, 0).astype(jnp.float32)
    block[:, width:] = digits.astype(jnp.bfloat16)
    if len(refs) == 5:
        normed_outs[0][...] = normed
        normed_outs[1][...] = normed
    else:
        keep_or_give(at[0], normed, refs[0][...], *normed_outs)


def keep_or_give(first, image, text, keep, give):
    keep[...] = jnp.where(first == 1, image, text)
    give[...] = jnp.where(first == 1, text, image)


def head_forward(at, hidden, labels, gain, shift, weight, text_normed=()):
    rows, width = hidden.shape
    vmem = pl.BlockSpec(memory_space=pltpu.VMEM)
    smem = pl.BlockSpec(memory_space=pltpu.SMEM)
    shape = jax.ShapeDtypeStruct
    wide = weight.shape[1] + label_base
    return pl.pallas_call(
        forward_kernel,
        out_shape=[
            shape((rows, wide), jnp.bfloat16),
            shape((rows, width), jnp.float32),
            shape((rows, wide), jnp.float32),
            shape((rows, width), jnp.bfloat16),
            shape((rows, width), jnp.bfloat16),
        ],
        in_specs=[smem] + [vmem] * (5 + len(text_normed)),
        out_specs=[vmem, pl.BlockSpec(), pl.BlockSpec(), vmem, vmem],
        compiler_params=pltpu.CompilerParams(vmem_limit_bytes=8 * 1024 * 1024),
    )(at, hidden, gain[None, :], shift[None, :], labels[None, :], weight, *text_normed)


def heads_kernel(count, at, img_kept, txt_kept, *refs):
    heads, keep, give = refs[-4:-2], refs[-2], refs[-1]
    for kept, terms, head in (
        (img_kept, refs[:count], heads[0]),
        (txt_kept, refs[count:-4], heads[1]),
    ):
        rows, width = head.shape
        unit, length = kept[:, :width], kept[:, width : width + 1]
        d_unit = sum(ref[:rows, :width].astype(jnp.float32) for ref in terms)
        projected = jnp.sum(unit * d_unit, axis=-1, keepdims=True)
        head[...] = ((d_unit - unit * projected) / length).astype(jnp.bfloat16)
    keep_or_give(at[0], heads[0][...], heads[1][...], keep, give)


def head_gradients(at, img_kept, txt_kept, img_terms, txt_terms):
    rows, width = img_kept.shape[0], img_kept.shape[1] - label_base
    vmem = pl.BlockSpec(memory_space=pltpu.VMEM)
    smem = pl.BlockSpec(memory_space=pltpu.SMEM)
    return pl.pallas_call(
        functools.partial(heads_kernel, len(img_terms)),
        out_shape=[jax.ShapeDtypeStruct((rows, width), jnp.bfloat16)] * 4,
        in_specs=[smem] + [vmem] * (2 + len(img_terms) + len(txt_terms)),
        out_specs=[vmem] * 4,
        compiler_params=pltpu.CompilerParams(vmem_limit_bytes=4 * 1024 * 1024),
    )(at, img_kept, txt_kept, *img_terms, *txt_terms)


def backward_kernel(head_grad, scaled, kept, gain, weight, out, held, arrived):
    width = scaled.shape[1]
    chunk = held.shape[0] // 8
    copies = []
    for i in range(8):
        part = pl.ds(chunk * i, chunk)
        copies.append(pltpu.make_async_copy(weight.at[part], held.at[part], arrived.at[i]))
        copies[-1].start()
    for copy in copies:
        copy.wait()
    inverse = kept[:, width + 1 : width + 2]
    d_normed = lax.dot_general(
        head_grad[...],
        held[...],
        (((1,), (1,)), ((), ())),
        preferred_element_type=jnp.float32,
    )
    weighted = d_normed * gain[...]
    first = jnp.mean(weighted, axis=-1, keepdims=True)
    second = jnp.mean(weighted * scaled[...], axis=-1, keepdims=True)
    out[...] = (inverse * (weighted - first - scaled[...] * second)).astype(jnp.bfloat16)


def norm_backward(head_grad, scaled, kept, gain, weight):
    vmem = pl.BlockSpec(memory_space=pltpu.VMEM)
    return pl.pallas_call(
        backward_kernel,
        out_shape=jax.ShapeDtypeStruct(scaled.shape, jnp.bfloat16),
        in_specs=[vmem] * 4 + [pl.BlockSpec(memory_space=pltpu.HBM)],
        scratch_shapes=[
            pltpu.VMEM(weight.shape, weight.dtype),
            pltpu.SemaphoreType.DMA((8,)),
        ],
        compiler_params=pltpu.CompilerParams(vmem_limit_bytes=8 * 1024 * 1024),
        cost_estimate=pl.CostEstimate(
            flops=2 * scaled.size * weight.shape[0], bytes_accessed=8 * 2**20, transcendentals=0
        ),
    )(head_grad, scaled, kept, gain[None, :], weight)


def weight_kernel(at, *refs):
    heads, normed, outs = refs[:4], refs[4:8], refs[8:]
    lanes = 8 * 128
    for out, by in zip(outs, (0, 1, 3, 2)):
        start = (at[2] + by) % 4 * 256
        total = None
        for head, piece in zip(heads, normed):
            from_lane = pl.multiple_of(start + piece.shape[1] - lanes, 128)
            rows = piece[:, pl.ds(from_lane, 256)]
            rows = jnp.concatenate([rows[:, :128], rows[:, 128:]], axis=0)
            term = jnp.dot(rows, head[...], preferred_element_type=jnp.float32)
            total = term if total is None else total + term
        out[...] = total.astype(jnp.bfloat16)


def weight_parts(at, heads, normed):
    width = heads[0].shape[1]
    vmem = pl.BlockSpec(memory_space=pltpu.VMEM)
    return pl.pallas_call(
        weight_kernel,
        out_shape=[jax.ShapeDtypeStruct((8 * piece_rows, width), jnp.bfloat16)] * 4,
        in_specs=[pl.BlockSpec(memory_space=pltpu.SMEM)] + [vmem] * 8,
        out_specs=[vmem] * 4,
        compiler_params=pltpu.CompilerParams(vmem_limit_bytes=4 * 1024 * 1024),
    )(at, *heads, *normed)


def pick_kernel(at, keep, got, *outs):
    first, at_first, z_at = at[0], at[1], at[3]
    width = keep.shape[1]
    short = width // 128
    normed = jnp.concatenate([keep[...], got[...]], axis=0)
    spot = lax.broadcasted_iota(jnp.int32, (8 * piece_rows, 1), 0)
    column = lax.broadcasted_iota(jnp.int32, (8 * piece_rows, width), 1)
    slot = spot // piece_rows
    inner = (slot ^ z_at) * short + spot % piece_rows
    for by, out in enumerate(outs):
        one = (at_first + by) % 4
        for two in range(4):
            by_x = two % 2 * 8 + one * 2 + two // 2
            by_y = one % 2 * 8 + two * 2 + one // 2
            row = jnp.where(first == 1, by_x, by_y) * (8 * short) + inner
            row = jnp.where(spot % piece_rows < short, row, -1)
            chosen = jnp.where(column == row, 1.0, 0.0).astype(jnp.bfloat16)
            picked = lax.dot_general(
                chosen, normed, (((1,), (1,)), ((), ())), preferred_element_type=jnp.float32
            ).astype(jnp.bfloat16)
            out[:, 256 * two : 256 * two + 128] = picked[:64, :]
            out[:, 256 * two + 128 : 256 * (two + 1)] = picked[64:, :]


def one_hot(rows, wanted):
    row = lax.broadcasted_iota(jnp.int32, (rows, wanted.shape[1]), 0)
    return jnp.where(row == wanted, 1.0, 0.0).astype(jnp.bfloat16)


def close_kernel(own, by_z, by_h, by_both, out):
    short = own.shape[1] // 128
    spot = lax.broadcasted_iota(jnp.int32, (1, piece_rows), 1)
    total = None
    for k, ref in enumerate((own, by_z, by_h, by_both)):
        chosen = one_hot(out.shape[0], jnp.where(spot < short, spot + k * short, -1))
        term = jnp.dot(chosen, ref[...], preferred_element_type=jnp.float32)
        total = term if total is None else total + term
    out[...] = total.astype(jnp.bfloat16)


def order_kernel(at, *refs):
    z_at, h_at = at[3], at[4]
    rows, width = refs[-1].shape
    short = rows // 16
    total = None
    for k, ref in enumerate(refs[:-1]):
        spot = lax.broadcasted_iota(jnp.int32, (1, ref.shape[0]), 1)
        piece = spot // short
        row = (z_at ^ 2 * k ^ piece % 2) * short + spot % short
        row = row + (h_at ^ piece // 2) * (8 * short)
        chosen = one_hot(rows, jnp.where(piece < 4, row, -1))
        term = jnp.dot(chosen, ref[...], preferred_element_type=jnp.float32)
        total = term if total is None else total + term
    refs[-1][...] = total.astype(jnp.bfloat16)


def close_rows(pieces, rows):
    vmem = pl.BlockSpec(memory_space=pltpu.VMEM)
    return pl.pallas_call(
        close_kernel,
        out_shape=jax.ShapeDtypeStruct((rows, pieces[0].shape[1]), jnp.bfloat16),
        in_specs=[vmem] * 4,
        out_specs=vmem,
        compiler_params=pltpu.CompilerParams(vmem_limit_bytes=3 * 1024 * 1024),
    )(*pieces)


def order_rows(at, slots, rows):
    vmem = pl.BlockSpec(memory_space=pltpu.VMEM)
    return pl.pallas_call(
        order_kernel,
        out_shape=jax.ShapeDtypeStruct((rows, slots[0].shape[1]), jnp.bfloat16),
        in_specs=[pl.BlockSpec(memory_space=pltpu.SMEM)] + [vmem] * 4,
        out_specs=vmem,
        compiler_params=pltpu.CompilerParams(vmem_limit_bytes=3 * 1024 * 1024),
    )(at, *slots)


def hop(block, z_by, h_by=0):
    return send(block, ("z", "h"), lambda at: {"z": at["z"] ^ z_by, "h": at["h"] ^ h_by})


def tie(*arrays):
    return lax.optimization_barrier(arrays)


def gather_units(txt_block, img_block, give_normed):
    up, down = send_z(txt_block, 1), send_z(txt_block, -1)
    near = [img_block] + [send(img_block, plane, plane_first(k)) for k in (1, 3, 2)]
    up, down = tie(up, down)
    mine = [txt_block, up, down]
    up, down = send_z(up, 1), send_z(down, -1)
    up, down, near = tie(up, down, jnp.concatenate(near))
    mine = [jnp.concatenate(mine + [up, down])]
    up, down = send_z(up, 1), send_z(down, -1)
    images = [near] + [send(near, plane, plane_second(k)) for k in (1, 2, 3)]
    other = [swap_core(mine[0])]
    got_normed = swap_core(give_normed)
    up, down, got_normed = tie(up, down, got_normed)
    mine.append(jnp.concatenate([up, down, send_z(up, 1)]))
    other.append(swap_core(mine[1]))
    return images, mine, other, got_normed


def scatter_units(img_parts, txt_mine, txt_other, pieces):
    rows = txt_mine.shape[0] // 8
    f32, bf16 = jnp.float32, jnp.bfloat16
    swapped, *img_parts = tie(swap_core(txt_other), *img_parts)
    away = [send(img_parts[k], plane, plane_second(-k)) for k in (1, 3, 2)]

    def part(i):
        at = slice(rows * i, rows * (i + 1))
        return txt_mine[at].astype(f32) + swapped[at].astype(f32)

    def onward(i, arrived):
        return (part(i) + arrived.astype(f32)).astype(bf16)

    low, one = tie(send_z(part(7).astype(bf16), -1), away[0])
    low, high = onward(5, low), part(6).astype(bf16)
    low, high = send_z(low, -1), send_z(high, 1)
    low, high, three = tie(low, high, away[1])
    low, high = onward(3, low), onward(4, high)
    low, high = send_z(low, -1), send_z(high, 1)
    low, high, two = tie(low, high, away[2])
    low, high = onward(1, low), onward(2, high)
    low, high = send_z(low, -1), send_z(high, 1)
    away = [one, three, two]
    near = img_parts[0].astype(f32) + sum(block.astype(f32) for block in away)
    img_terms = [near[:rows]]
    for i, k in enumerate((1, 3, 2)):
        block = near[rows * (i + 1) : rows * (i + 2)].astype(bf16)
        block = jnp.concatenate([block, pieces[(4 - k) % 4]], axis=1)
        img_terms.append(send(block, plane, plane_first(-k)))
    return img_terms, [txt_mine, swapped, low, high]


def send_z(block, by):
    return send(block, ("z",), along("z", by))


def pair_kernel(consts, *refs):
    images, texts = refs[:4], refs[4:8]
    pair_ref, all_ref, mine_ref, other_ref, digits, total = refs[8:]
    width = all_ref.shape[1]
    step = images[0].shape[0]
    scale, offset, size = consts[0], consts[1], consts[2]
    at = 0
    for ref in texts:
        rows = ref.shape[0]
        all_ref[at : at + rows, :] = ref[:, :width]
        digits[at : at + rows, :] = ref[:, width:].astype(jnp.float32)
        at += rows
    for q in range(4):
        here = slice(step * q, step * (q + 1))
        text = all_ref[here, :]
        turned = digits[here, :].T
        txt_ids = turned[0:1, :] * label_base + turned[1:2, :]
        for j in range(4):
            image = images[j][:, :width]
            below = images[j][:, width:].astype(jnp.float32)
            img_ids = below[:, 0:1] * label_base + below[:, 1:2]
            dots = lax.dot_general(
                image, text, (((1,), (1,)), ((), ())), preferred_element_type=jnp.float32
            )
            logits = dots * scale + offset
            match = img_ids == txt_ids
            ratio = 1.0 / (1.0 + jnp.exp(jnp.where(match, logits, -logits)))
            pair = (jnp.where(match, -size, size) * ratio).astype(jnp.bfloat16)
            pair_ref[step * j : step * (j + 1), here] = pair
            part = lax.dot_general(
                pair, image, (((0,), (0,)), ((), ())), preferred_element_type=jnp.float32
            )
            if j == 0:
                total[...] = part
            else:
                total[...] += part
        out_ref = (mine_ref, other_ref)[q // 2]
        out_ref[step * (q % 2) : step * (q % 2 + 1), :] = total[...].astype(jnp.bfloat16)


def image_kernel(at, pair_ref, all_ref, keep, got, *outs):
    step = outs[0].shape[0]
    for j in range(4):
        outs[j][...] = jnp.dot(
            pair_ref[step * j : step * (j + 1), :],
            all_ref[...],
            preferred_element_type=jnp.float32,
        ).astype(jnp.bfloat16)
    pick_kernel(at, keep, got, *outs[4:])


def pair_products(images, mine, other, consts, at, keep, got):
    rows, width = keep.shape
    step = images[0].shape[0]
    count = 4 * step
    vmem = pl.BlockSpec(memory_space=pltpu.VMEM)
    params = pltpu.CompilerParams(vmem_limit_bytes=6 * 1024 * 1024)
    shape = functools.partial(jax.ShapeDtypeStruct, dtype=jnp.bfloat16)
    pair, texts, txt_mine, txt_other = pl.pallas_call(
        pair_kernel,
        out_shape=[
            shape((count, count)),
            shape((count, width)),
            shape((count // 2, width)),
            shape((count // 2, width)),
        ],
        in_specs=[pl.BlockSpec(memory_space=pltpu.SMEM)] + [vmem] * 8,
        out_specs=[vmem] * 4,
        scratch_shapes=[
            pltpu.VMEM((count, label_base), jnp.float32),
            pltpu.VMEM((step, width), jnp.float32),
        ],
        compiler_params=params,
        cost_estimate=pl.CostEstimate(
            flops=4 * count * count * width, bytes_accessed=12 * 2**20, transcendentals=2 * count**2
        ),
    )(consts, *images, *mine, *other)
    parts = pl.pallas_call(
        image_kernel,
        out_shape=[shape((step, width))] * 4 + [shape((rows, 8 * 128))] * 4,
        in_specs=[pl.BlockSpec(memory_space=pltpu.SMEM)] + [vmem] * 4,
        out_specs=[vmem] * 8,
        compiler_params=pltpu.CompilerParams(vmem_limit_bytes=8 * 1024 * 1024),
        cost_estimate=pl.CostEstimate(
            flops=2 * count * count * width, bytes_accessed=8 * 2**20, transcendentals=0
        ),
    )(at, pair, texts, keep, got)
    return parts[:4], parts[4:], txt_mine, txt_other


def shards(
    img_hidden,
    txt_hidden,
    img_labels,
    txt_labels,
    img_gain,
    img_shift,
    txt_gain,
    txt_shift,
    img_weight,
    txt_weight,
    logit_scale,
    logit_bias,
    loss_scale,
    row_moment,
    col_moment,
):
    rows, width = img_hidden.shape
    depth = img_weight.shape[0]
    first = lax.axis_index("c") == 0
    x_at = lax.axis_index("x")
    y_at = lax.axis_index("h") * 2 + lax.axis_index("l")
    at = [
        1 - lax.axis_index("c"),
        jnp.where(first, x_at, y_at),
        jnp.where(first, y_at, x_at),
        lax.axis_index("z"),
        lax.axis_index("h"),
    ]
    consts = [logit_scale[0], logit_bias[0], loss_scale[0] * logit_scale[0]]
    at, consts, txt_hidden = tie(jnp.stack(at), jnp.stack(consts), txt_hidden)

    txt_block, txt_scaled, txt_kept, txt_normed, _ = head_forward(
        at, txt_hidden, txt_labels, txt_gain, txt_shift, txt_weight
    )
    txt_block, img_hidden = tie(txt_block, img_hidden)
    img_block, img_scaled, img_kept, keep_normed, give_normed = head_forward(
        at, img_hidden, img_labels, img_gain, img_shift, img_weight, (txt_normed,)
    )
    images, mine, other, got_normed = gather_units(txt_block, img_block, give_normed)
    img_parts, pieces, txt_mine, txt_other = pair_products(
        images,
        mine,
        other,
        consts,
        at,
        keep_normed,
        got_normed,
    )
    img_terms, txt_terms = scatter_units(img_parts, txt_mine, txt_other, pieces)
    img_head, txt_head, keep_head, give_head = head_gradients(
        at, img_kept, txt_kept, img_terms, txt_terms
    )
    img_grad = norm_backward(img_head, img_scaled, img_kept, img_gain, img_weight)
    txt_grad = norm_backward(txt_head, txt_scaled, txt_kept, txt_gain, txt_weight)
    head = jnp.concatenate([keep_head, swap_core(give_head)])
    heads = [head] + [send(head, plane, plane_first(-k)) for k in (1, 3, 2)]
    own, *away = weight_parts(at, heads, [pieces[0]] + img_terms[1:])
    total = own.astype(jnp.float32)
    for k, block in zip((1, 3, 2), away):
        total = total + send(block, plane, plane_second(k)).astype(jnp.float32)
    total = total.astype(jnp.bfloat16)
    sent = [hop(total[32 * i : 32 * (i + 1)], 2 * i) for i in (1, 2, 3)]
    total = total[:32].astype(jnp.float32) + sum(block.astype(jnp.float32) for block in sent)
    total = total.astype(jnp.bfloat16)
    total = total[:16].astype(jnp.float32) + hop(total[16:], 1).astype(jnp.float32)
    total = total.astype(jnp.bfloat16)
    four = close_rows([total, hop(total, 1), hop(total, 0, 1), hop(total, 1, 1)], 48)
    slots = [four] + [hop(four, k) for k in (2, 4, 6)]
    total = order_rows(at, slots, depth // 8)
    other = swap_core(total)
    towers = [jnp.where(first, total, other), jnp.where(first, other, total)]
    towers = [grads.astype(jnp.float32) for grads in towers]

    squares = [grads * grads for grads in towers]
    row_means = jnp.stack([jnp.mean(square, axis=1) for square in squares])
    row_new = second_decay * row_moment + (1.0 - second_decay) * row_means
    row_sums = jnp.pad(jnp.sum(row_new, axis=1)[:, None], ((0, 0), (0, 127)))
    col_sums = jnp.stack([jnp.sum(square, axis=0) for square in squares])
    sums = jnp.concatenate([col_sums, row_sums], axis=1)
    sums = jnp.broadcast_to(sums[None], (8,) + sums.shape)
    sums = jnp.sum(lax.all_to_all(sums, txt_axes, 0, 0, tiled=True), axis=0)
    col_new = second_decay * col_moment + (1.0 - second_decay) * (sums[:, :width] / depth)
    row_mean = sums[:, width] / depth
    update = jnp.concatenate(
        [
            towers[k] / jnp.sqrt(row_new[k][:, None] * col_new[k][None, :] / row_mean[k])
            for k in (0, 1)
        ],
        axis=1,
    )
    return (img_grad, txt_grad, update, row_new, col_new)


def solution(mesh):
    fine = Mesh(mesh.devices.reshape([sizes[a] for a in every]), every)
    whole = P()
    in_specs = (rows_spec,) * 4 + (whole,) * 9 + (P(None, txt_axes), whole)
    out_specs = (rows_spec, rows_spec, P(txt_axes), P(None, txt_axes), whole)
    return jax.shard_map(shards, mesh=fine, in_specs=in_specs, out_specs=out_specs, check_vma=False)
```

```python
import functools
import itertools

import jax
import jax.numpy as jnp
from jax import lax
from jax.experimental import pallas as pl
from jax.experimental.pallas import tpu as pltpu
from jax.sharding import Mesh
from jax.sharding import PartitionSpec as P

norm_eps = 1e-06
second_decay = 0.6
label_base = 128
piece_rows = 16
sizes = {"z": 8, "h": 2, "c": 2, "l": 2, "x": 4}
every = ("z", "h", "c", "l", "x")
rows_spec = P(every)
txt_axes = ("l", "x")


def route(axes, move):
    spots = list(itertools.product(*[range(sizes[a]) for a in axes]))
    index = {spot: i for i, spot in enumerate(spots)}
    pairs = []
    for spot in spots:
        there = move(dict(zip(axes, spot)))
        pairs.append((index[spot], index[tuple(there[a] % sizes[a] for a in axes)]))
    return pairs


def send(block, axes, move):
    return lax.ppermute(block, axes, route(axes, move))


def along(axis, by):
    return lambda at: {axis: at[axis] + by}


def turn_y(at, by):
    y = (at["h"] * 2 + at["l"] + by) % 4
    return {**at, "h": y // 2, "l": y % 2}


def turn_x(at, by):
    return {**at, "x": at["x"] + by}


plane = ("h", "c", "l", "x")


def plane_first(by):
    return lambda at: turn_x(at, by) if at["c"] == 0 else turn_y(at, by)


def plane_second(by):
    return lambda at: turn_y(at, by) if at["c"] == 0 else turn_x(at, by)


def swap_core(block):
    return send(block, ("c",), along("c", 1))


def forward_kernel(at, hidden, gain, shift, labels, weight, *refs):
    rows, width = hidden.shape
    block, scaled, kept, normed_outs = refs[-5], refs[-4], refs[-3], refs[-2:]
    values = hidden[...].astype(jnp.float32)
    center = jnp.mean(values, axis=-1, keepdims=True)
    spread = jnp.mean(jnp.square(values - center), axis=-1, keepdims=True)
    inverse = lax.rsqrt(spread + norm_eps)
    scaled[...] = (values - center) * inverse
    normed = (scaled[...] * gain[...] + shift[...]).astype(jnp.bfloat16)
    embed = jnp.dot(normed, weight[...], preferred_element_type=jnp.float32)
    length = jnp.sqrt(jnp.sum(embed * embed, axis=-1, keepdims=True))
    unit = embed / length
    kept[:, :width] = unit
    lane = lax.broadcasted_iota(jnp.int32, (rows, label_base), 1)
    kept[:, width:] = jnp.where(lane == 0, length, inverse)
    block[:, :width] = unit.astype(jnp.bfloat16)
    one, two = (lax.broadcasted_iota(jnp.int32, (rows, rows), d) for d in (0, 1))
    column = jnp.where(one == two, labels[...], 0).astype(jnp.float32)
    column = jnp.sum(column, axis=1, keepdims=True).astype(jnp.int32)
    digits = jnp.where(lane == 0, column // label_base, column % label_base)
    digits = jnp.where(lane < 2, digits, 0).astype(jnp.float32)
    block[:, width:] = digits.astype(jnp.bfloat16)
    if len(refs) == 5:
        normed_outs[0][...] = normed
        normed_outs[1][...] = normed
    else:
        keep_or_give(at[0], normed, refs[0][...], *normed_outs)


def keep_or_give(first, image, text, keep, give):
    keep[...] = jnp.where(first == 1, image, text)
    give[...] = jnp.where(first == 1, text, image)


def head_forward(at, hidden, labels, gain, shift, weight, text_normed=()):
    rows, width = hidden.shape
    vmem = pl.BlockSpec(memory_space=pltpu.VMEM)
    smem = pl.BlockSpec(memory_space=pltpu.SMEM)
    shape = jax.ShapeDtypeStruct
    wide = weight.shape[1] + label_base
    return pl.pallas_call(
        forward_kernel,
        out_shape=[
            shape((rows, wide), jnp.bfloat16),
            shape((rows, width), jnp.float32),
            shape((rows, wide), jnp.float32),
            shape((rows, width), jnp.bfloat16),
            shape((rows, width), jnp.bfloat16),
        ],
        in_specs=[smem] + [vmem] * (5 + len(text_normed)),
        out_specs=[vmem, pl.BlockSpec(), pl.BlockSpec(), vmem, vmem],
        compiler_params=pltpu.CompilerParams(vmem_limit_bytes=8 * 1024 * 1024),
    )(at, hidden, gain[None, :], shift[None, :], labels[None, :], weight, *text_normed)


def heads_kernel(count, at, img_kept, txt_kept, *refs):
    heads, keep, give = refs[-4:-2], refs[-2], refs[-1]
    for kept, terms, head in (
        (img_kept, refs[:count], heads[0]),
        (txt_kept, refs[count:-4], heads[1]),
    ):
        rows, width = head.shape
        unit, length = kept[:, :width], kept[:, width : width + 1]
        d_unit = sum(ref[:rows, :width].astype(jnp.float32) for ref in terms)
        projected = jnp.sum(unit * d_unit, axis=-1, keepdims=True)
        head[...] = ((d_unit - unit * projected) / length).astype(jnp.bfloat16)
    keep_or_give(at[0], heads[0][...], heads[1][...], keep, give)


def head_gradients(at, img_kept, txt_kept, img_terms, txt_terms):
    rows, width = img_kept.shape[0], img_kept.shape[1] - label_base
    vmem = pl.BlockSpec(memory_space=pltpu.VMEM)
    smem = pl.BlockSpec(memory_space=pltpu.SMEM)
    return pl.pallas_call(
        functools.partial(heads_kernel, len(img_terms)),
        out_shape=[jax.ShapeDtypeStruct((rows, width), jnp.bfloat16)] * 4,
        in_specs=[smem] + [vmem] * (2 + len(img_terms) + len(txt_terms)),
        out_specs=[vmem] * 4,
        compiler_params=pltpu.CompilerParams(vmem_limit_bytes=4 * 1024 * 1024),
    )(at, img_kept, txt_kept, *img_terms, *txt_terms)


def backward_kernel(head_grad, scaled, kept, gain, weight, out):
    width = scaled.shape[1]
    inverse = kept[:, width + 1 : width + 2]
    d_normed = lax.dot_general(
        head_grad[...],
        weight[...],
        (((1,), (1,)), ((), ())),
        preferred_element_type=jnp.float32,
    )
    weighted = d_normed * gain[...]
    first = jnp.mean(weighted, axis=-1, keepdims=True)
    second = jnp.mean(weighted * scaled[...], axis=-1, keepdims=True)
    out[...] = (inverse * (weighted - first - scaled[...] * second)).astype(jnp.bfloat16)


def norm_backward(head_grad, scaled, kept, gain, weight):
    return pl.pallas_call(
        backward_kernel,
        out_shape=jax.ShapeDtypeStruct(scaled.shape, jnp.bfloat16),
        compiler_params=pltpu.CompilerParams(vmem_limit_bytes=8 * 1024 * 1024),
        cost_estimate=pl.CostEstimate(
            flops=2 * scaled.size * weight.shape[0], bytes_accessed=8 * 2**20, transcendentals=0
        ),
    )(head_grad, scaled, kept, gain[None, :], weight)


def weight_kernel(at, *refs):
    heads, normed, outs = refs[:4], refs[4:8], refs[8:]
    lanes = 8 * 128
    for out, by in zip(outs, (0, 1, 3, 2)):
        start = (at[2] + by) % 4 * 256
        total = None
        for head, piece in zip(heads, normed):
            from_lane = pl.multiple_of(start + piece.shape[1] - lanes, 128)
            rows = piece[:, pl.ds(from_lane, 256)]
            rows = jnp.concatenate([rows[:, :128], rows[:, 128:]], axis=0)
            term = jnp.dot(rows, head[...], preferred_element_type=jnp.float32)
            total = term if total is None else total + term
        out[...] = total.astype(jnp.bfloat16)


def weight_parts(at, heads, normed):
    width = heads[0].shape[1]
    vmem = pl.BlockSpec(memory_space=pltpu.VMEM)
    return pl.pallas_call(
        weight_kernel,
        out_shape=[jax.ShapeDtypeStruct((8 * piece_rows, width), jnp.bfloat16)] * 4,
        in_specs=[pl.BlockSpec(memory_space=pltpu.SMEM)] + [vmem] * 8,
        out_specs=[vmem] * 4,
        compiler_params=pltpu.CompilerParams(vmem_limit_bytes=4 * 1024 * 1024),
    )(at, *heads, *normed)


def pick_kernel(at, keep, got, *outs):
    first, at_first, z_at = at[0], at[1], at[3]
    width = keep.shape[1]
    short = width // 128
    normed = jnp.concatenate([keep[...], got[...]], axis=0)
    spot = lax.broadcasted_iota(jnp.int32, (8 * piece_rows, 1), 0)
    column = lax.broadcasted_iota(jnp.int32, (8 * piece_rows, width), 1)
    slot = spot // piece_rows
    inner = (slot ^ z_at) * short + spot % piece_rows
    for by, out in enumerate(outs):
        one = (at_first + by) % 4
        for two in range(4):
            by_x = two % 2 * 8 + one * 2 + two // 2
            by_y = one % 2 * 8 + two * 2 + one // 2
            row = jnp.where(first == 1, by_x, by_y) * (8 * short) + inner
            row = jnp.where(spot % piece_rows < short, row, -1)
            chosen = jnp.where(column == row, 1.0, 0.0).astype(jnp.bfloat16)
            picked = lax.dot_general(
                chosen, normed, (((1,), (1,)), ((), ())), preferred_element_type=jnp.float32
            ).astype(jnp.bfloat16)
            out[:, 256 * two : 256 * two + 128] = picked[:64, :]
            out[:, 256 * two + 128 : 256 * (two + 1)] = picked[64:, :]


def one_hot(rows, wanted):
    row = lax.broadcasted_iota(jnp.int32, (rows, wanted.shape[1]), 0)
    return jnp.where(row == wanted, 1.0, 0.0).astype(jnp.bfloat16)


def close_kernel(own, by_z, by_h, by_both, out):
    short = own.shape[1] // 128
    spot = lax.broadcasted_iota(jnp.int32, (1, piece_rows), 1)
    total = None
    for k, ref in enumerate((own, by_z, by_h, by_both)):
        chosen = one_hot(out.shape[0], jnp.where(spot < short, spot + k * short, -1))
        term = jnp.dot(chosen, ref[...], preferred_element_type=jnp.float32)
        total = term if total is None else total + term
    out[...] = total.astype(jnp.bfloat16)


def order_kernel(at, *refs):
    z_at, h_at = at[3], at[4]
    rows, width = refs[-1].shape
    short = rows // 16
    total = None
    for k, ref in enumerate(refs[:-1]):
        spot = lax.broadcasted_iota(jnp.int32, (1, ref.shape[0]), 1)
        piece = spot // short
        row = (z_at ^ 2 * k ^ piece % 2) * short + spot % short
        row = row + (h_at ^ piece // 2) * (8 * short)
        chosen = one_hot(rows, jnp.where(piece < 4, row, -1))
        term = jnp.dot(chosen, ref[...], preferred_element_type=jnp.float32)
        total = term if total is None else total + term
    refs[-1][...] = total.astype(jnp.bfloat16)


def close_rows(pieces, rows):
    vmem = pl.BlockSpec(memory_space=pltpu.VMEM)
    return pl.pallas_call(
        close_kernel,
        out_shape=jax.ShapeDtypeStruct((rows, pieces[0].shape[1]), jnp.bfloat16),
        in_specs=[vmem] * 4,
        out_specs=vmem,
        compiler_params=pltpu.CompilerParams(vmem_limit_bytes=3 * 1024 * 1024),
    )(*pieces)


def order_rows(at, slots, rows):
    vmem = pl.BlockSpec(memory_space=pltpu.VMEM)
    return pl.pallas_call(
        order_kernel,
        out_shape=jax.ShapeDtypeStruct((rows, slots[0].shape[1]), jnp.bfloat16),
        in_specs=[pl.BlockSpec(memory_space=pltpu.SMEM)] + [vmem] * 4,
        out_specs=vmem,
        compiler_params=pltpu.CompilerParams(vmem_limit_bytes=3 * 1024 * 1024),
    )(at, *slots)


def hop(block, z_by, h_by=0):
    return send(block, ("z", "h"), lambda at: {"z": at["z"] ^ z_by, "h": at["h"] ^ h_by})


def tie(*arrays):
    return lax.optimization_barrier(arrays)


def gather_units(txt_block, img_block, give_normed):
    up, down = send_z(txt_block, 1), send_z(txt_block, -1)
    near = [img_block] + [send(img_block, plane, plane_first(k)) for k in (1, 3, 2)]
    up, down = tie(up, down)
    mine = [txt_block, up, down]
    up, down = send_z(up, 1), send_z(down, -1)
    up, down, near = tie(up, down, jnp.concatenate(near))
    mine = [jnp.concatenate(mine + [up, down])]
    up, down = send_z(up, 1), send_z(down, -1)
    images = [near] + [send(near, plane, plane_second(k)) for k in (1, 2, 3)]
    other = [swap_core(mine[0])]
    got_normed = swap_core(give_normed)
    up, down, got_normed = tie(up, down, got_normed)
    mine.append(jnp.concatenate([up, down, send_z(up, 1)]))
    other.append(swap_core(mine[1]))
    return images, mine, other, got_normed


def scatter_units(img_parts, txt_mine, txt_other, pieces):
    rows = txt_mine.shape[0] // 8
    f32, bf16 = jnp.float32, jnp.bfloat16
    swapped, *img_parts = tie(swap_core(txt_other), *img_parts)
    away = [send(img_parts[k], plane, plane_second(-k)) for k in (1, 3, 2)]

    def part(i):
        at = slice(rows * i, rows * (i + 1))
        return txt_mine[at].astype(f32) + swapped[at].astype(f32)

    def onward(i, arrived):
        return (part(i) + arrived.astype(f32)).astype(bf16)

    low, one = tie(send_z(part(7).astype(bf16), -1), away[0])
    low, high = onward(5, low), part(6).astype(bf16)
    low, high = send_z(low, -1), send_z(high, 1)
    low, high, three = tie(low, high, away[1])
    low, high = onward(3, low), onward(4, high)
    low, high = send_z(low, -1), send_z(high, 1)
    low, high = tie(low, high)
    low, high = onward(1, low), onward(2, high)
    low, high = send_z(low, -1), send_z(high, 1)
    away = [one, three, away[2]]
    near = img_parts[0].astype(f32) + sum(block.astype(f32) for block in away)
    img_terms = [near[:rows]]
    for i, k in enumerate((1, 3, 2)):
        block = near[rows * (i + 1) : rows * (i + 2)].astype(bf16)
        block = jnp.concatenate([block, pieces[(4 - k) % 4]], axis=1)
        img_terms.append(send(block, plane, plane_first(-k)))
    return img_terms, [txt_mine, swapped, low, high]


def send_z(block, by):
    return send(block, ("z",), along("z", by))


def pair_kernel(consts, *refs):
    images, texts = refs[:4], refs[4:8]
    pair_ref, all_ref, mine_ref, other_ref, digits, total = refs[8:]
    width = all_ref.shape[1]
    step = images[0].shape[0]
    scale, offset, size = consts[0], consts[1], consts[2]
    at = 0
    for ref in texts:
        rows = ref.shape[0]
        all_ref[at : at + rows, :] = ref[:, :width]
        digits[at : at + rows, :] = ref[:, width:].astype(jnp.float32)
        at += rows
    for q in range(4):
        here = slice(step * q, step * (q + 1))
        text = all_ref[here, :]
        turned = digits[here, :].T
        txt_ids = turned[0:1, :] * label_base + turned[1:2, :]
        for j in range(4):
            image = images[j][:, :width]
            below = images[j][:, width:].astype(jnp.float32)
            img_ids = below[:, 0:1] * label_base + below[:, 1:2]
            dots = lax.dot_general(
                image, text, (((1,), (1,)), ((), ())), preferred_element_type=jnp.float32
            )
            logits = dots * scale + offset
            match = img_ids == txt_ids
            ratio = 1.0 / (1.0 + jnp.exp(jnp.where(match, logits, -logits)))
            pair = (jnp.where(match, -size, size) * ratio).astype(jnp.bfloat16)
            pair_ref[step * j : step * (j + 1), here] = pair
            part = lax.dot_general(
                pair, image, (((0,), (0,)), ((), ())), preferred_element_type=jnp.float32
            )
            if j == 0:
                total[...] = part
            else:
                total[...] += part
        out_ref = (mine_ref, other_ref)[q // 2]
        out_ref[step * (q % 2) : step * (q % 2 + 1), :] = total[...].astype(jnp.bfloat16)


def image_kernel(at, pair_ref, all_ref, keep, got, *outs):
    step = outs[0].shape[0]
    for j in range(4):
        outs[j][...] = jnp.dot(
            pair_ref[step * j : step * (j + 1), :],
            all_ref[...],
            preferred_element_type=jnp.float32,
        ).astype(jnp.bfloat16)
    pick_kernel(at, keep, got, *outs[4:])


def pair_products(images, mine, other, consts, at, keep, got):
    rows, width = keep.shape
    step = images[0].shape[0]
    count = 4 * step
    vmem = pl.BlockSpec(memory_space=pltpu.VMEM)
    params = pltpu.CompilerParams(vmem_limit_bytes=6 * 1024 * 1024)
    shape = functools.partial(jax.ShapeDtypeStruct, dtype=jnp.bfloat16)
    pair, texts, txt_mine, txt_other = pl.pallas_call(
        pair_kernel,
        out_shape=[
            shape((count, count)),
            shape((count, width)),
            shape((count // 2, width)),
            shape((count // 2, width)),
        ],
        in_specs=[pl.BlockSpec(memory_space=pltpu.SMEM)] + [vmem] * 8,
        out_specs=[vmem] * 4,
        scratch_shapes=[
            pltpu.VMEM((count, label_base), jnp.float32),
            pltpu.VMEM((step, width), jnp.float32),
        ],
        compiler_params=params,
        cost_estimate=pl.CostEstimate(
            flops=4 * count * count * width, bytes_accessed=12 * 2**20, transcendentals=2 * count**2
        ),
    )(consts, *images, *mine, *other)
    parts = pl.pallas_call(
        image_kernel,
        out_shape=[shape((step, width))] * 4 + [shape((rows, 8 * 128))] * 4,
        in_specs=[pl.BlockSpec(memory_space=pltpu.SMEM)] + [vmem] * 4,
        out_specs=[vmem] * 8,
        compiler_params=pltpu.CompilerParams(vmem_limit_bytes=8 * 1024 * 1024),
        cost_estimate=pl.CostEstimate(
            flops=2 * count * count * width, bytes_accessed=8 * 2**20, transcendentals=0
        ),
    )(at, pair, texts, keep, got)
    return parts[:4], parts[4:], txt_mine, txt_other


def shards(
    img_hidden,
    txt_hidden,
    img_labels,
    txt_labels,
    img_gain,
    img_shift,
    txt_gain,
    txt_shift,
    img_weight,
    txt_weight,
    logit_scale,
    logit_bias,
    loss_scale,
    row_moment,
    col_moment,
):
    rows, width = img_hidden.shape
    depth = img_weight.shape[0]
    first = lax.axis_index("c") == 0
    x_at = lax.axis_index("x")
    y_at = lax.axis_index("h") * 2 + lax.axis_index("l")
    at = [
        1 - lax.axis_index("c"),
        jnp.where(first, x_at, y_at),
        jnp.where(first, y_at, x_at),
        lax.axis_index("z"),
        lax.axis_index("h"),
    ]
    consts = [logit_scale[0], logit_bias[0], loss_scale[0] * logit_scale[0]]
    at, consts, txt_hidden = tie(jnp.stack(at), jnp.stack(consts), txt_hidden)

    txt_block, txt_scaled, txt_kept, txt_normed, _ = head_forward(
        at, txt_hidden, txt_labels, txt_gain, txt_shift, txt_weight
    )
    txt_block, img_hidden = tie(txt_block, img_hidden)
    img_block, img_scaled, img_kept, keep_normed, give_normed = head_forward(
        at, img_hidden, img_labels, img_gain, img_shift, img_weight, (txt_normed,)
    )
    images, mine, other, got_normed = gather_units(txt_block, img_block, give_normed)
    img_parts, pieces, txt_mine, txt_other = pair_products(
        images,
        mine,
        other,
        consts,
        at,
        keep_normed,
        got_normed,
    )
    img_terms, txt_terms = scatter_units(img_parts, txt_mine, txt_other, pieces)
    img_head, txt_head, keep_head, give_head = head_gradients(
        at, img_kept, txt_kept, img_terms, txt_terms
    )
    img_grad = norm_backward(img_head, img_scaled, img_kept, img_gain, img_weight)
    txt_grad = norm_backward(txt_head, txt_scaled, txt_kept, txt_gain, txt_weight)
    head = jnp.concatenate([keep_head, swap_core(give_head)])
    heads = [head] + [send(head, plane, plane_first(-k)) for k in (1, 3, 2)]
    own, *away = weight_parts(at, heads, [pieces[0]] + img_terms[1:])
    total = own.astype(jnp.float32)
    for k, block in zip((1, 3, 2), away):
        total = total + send(block, plane, plane_second(k)).astype(jnp.float32)
    total = total.astype(jnp.bfloat16)
    sent = [hop(total[32 * i : 32 * (i + 1)], 2 * i) for i in (1, 2, 3)]
    total = total[:32].astype(jnp.float32) + sum(block.astype(jnp.float32) for block in sent)
    total = total.astype(jnp.bfloat16)
    total = total[:16].astype(jnp.float32) + hop(total[16:], 1).astype(jnp.float32)
    total = total.astype(jnp.bfloat16)
    four = close_rows([total, hop(total, 1), hop(total, 0, 1), hop(total, 1, 1)], 48)
    slots = [four] + [hop(four, k) for k in (2, 4, 6)]
    total = order_rows(at, slots, depth // 8)
    other = swap_core(total)
    towers = [jnp.where(first, total, other), jnp.where(first, other, total)]
    towers = [grads.astype(jnp.float32) for grads in towers]

    squares = [grads * grads for grads in towers]
    row_means = jnp.stack([jnp.mean(square, axis=1) for square in squares])
    row_new = second_decay * row_moment + (1.0 - second_decay) * row_means
    row_sums = jnp.pad(jnp.sum(row_new, axis=1)[:, None], ((0, 0), (0, 127)))
    col_sums = jnp.stack([jnp.sum(square, axis=0) for square in squares])
    sums = jnp.concatenate([col_sums, row_sums], axis=1)
    sums = jnp.broadcast_to(sums[None], (8,) + sums.shape)
    sums = jnp.sum(lax.all_to_all(sums, txt_axes, 0, 0, tiled=True), axis=0)
    col_new = second_decay * col_moment + (1.0 - second_decay) * (sums[:, :width] / depth)
    row_mean = sums[:, width] / depth
    update = jnp.concatenate(
        [
            towers[k] / jnp.sqrt(row_new[k][:, None] * col_new[k][None, :] / row_mean[k])
            for k in (0, 1)
        ],
        axis=1,
    )
    return (img_grad, txt_grad, update, row_new, col_new)


def solution(mesh):
    fine = Mesh(mesh.devices.reshape([sizes[a] for a in every]), every)
    whole = P()
    in_specs = (rows_spec,) * 4 + (whole,) * 9 + (P(None, txt_axes), whole)
    out_specs = (rows_spec, rows_spec, P(txt_axes), P(None, txt_axes), whole)
    return jax.shard_map(shards, mesh=fine, in_specs=in_specs, out_specs=out_specs, check_vma=False)
```
